128 devices in a mesh: band: 16 (over y, z_lo, core), grid: 8 (over z_hi, x).
Axes of the slice: x: 4, y: 4, z: 4 (z_hi: 2, z_lo: 2; z = z_hi * 2 + z_lo), core: 2. Of those that a mesh axis runs over, the one named last changes fastest.
Arguments:
- orbitals: bfloat16 [32, 144, 144, 144], P('band', 'grid'), may hold values from -6 to 6
Outputs:
- exchange_terms: float32 [32, 144, 144, 144], P('band', 'grid')
The draws below stay inside these ranges and needn't reach their ends.
All inputs are finite; a program needn't handle non-finite values.
Results may differ from the reference program's by a relative error of at most 0.0003.
Values may be sent and summed in bfloat16 or wider, within the bound.
No kernel may reach another device: no remote copies, remote signals or barrier semaphores. Data moves between devices by JAX's collectives and lax.ppermute only.
A program may use at most 128 MiB of HBM per device.

```python
import math
import jax
import jax.numpy as jnp
from jax import lax

NG = 144
NBLK = 2
BANDS = 32
N_BAND = 16


def level_of(key, extent, cuts, low, high):
    def one(position, parts):
        draws = jax.random.uniform(jax.random.fold_in(jax.random.fold_in(key, 6), position), (parts,), jnp.float32, low / len(cuts), high / len(cuts))
        return jnp.repeat(jnp.exp(draws), extent[position] // parts).reshape((-1,) + (1,) * (len(extent) - position - 1))

    factor_of = one(*cuts[0])
    for cut in cuts[1:]:
        factor_of = factor_of * one(*cut)
    return factor_of


def gaussian(key, dims, deviation, bound, shards=(), held_as=jnp.bfloat16):
    factor_of = level_of(key, dims, shards, -0.22, 0.18) if shards else 1.0
    values = jax.random.normal(key, dims, jnp.float32) * deviation * factor_of
    return jnp.minimum(jnp.maximum(values, -bound), bound).astype(held_as)


def setup_inputs(seed: int = 0) -> dict:
    arg_keys = jax.random.split(jax.random.key(seed), 2)
    return {
        "orbitals": gaussian(arg_keys[0], (BANDS, NG, NG, NG), 1.0, 6.0, ((0, 16), (1, 8))),
    }


OMEGA = 0.5


def signed_freq(values, grid_len):
    return jnp.where(values <= grid_len // 2, values, values - grid_len)


def coulomb(freq_sq, grid_len):
    scale = (2.0 * math.pi / grid_len) ** 2
    g_sq = freq_sq.astype(jnp.float32) * jnp.float32(scale)
    safe_sq = jnp.where(freq_sq > 0, g_sq, jnp.float32(1.0))
    values = jnp.where(freq_sq > 0, 4.0 * math.pi / safe_sq * (1.0 - jnp.exp(-safe_sq / (4.0 * OMEGA * OMEGA))), jnp.float32(math.pi / (OMEGA * OMEGA)))
    return jnp.where(freq_sq <= (grid_len // 2) ** 2, values, jnp.float32(0.0))


def half_kernel(grid_len):
    full_idx = signed_freq(jnp.arange(grid_len, dtype=jnp.int32), grid_len)
    half_idx = jnp.arange(grid_len // 2 + 1, dtype=jnp.int32)
    freq_sq = full_idx[:, None, None] ** 2 + full_idx[None, :, None] ** 2 + half_idx[None, None, :] ** 2
    return coulomb(freq_sq, grid_len)


def reference(orbitals):
    phi = orbitals.astype(jnp.float32).reshape(N_BAND, NBLK, NG, NG, NG)
    kernel = half_kernel(NG)

    def group_step(block_idx):
        own_block = lax.dynamic_index_in_dim(phi, block_idx, 0, keepdims=False)
        lower_idx = ((block_idx + N_BAND - 1) % N_BAND).astype(jnp.int32)
        lower_block = lax.dynamic_index_in_dim(phi, lower_idx, 0, keepdims=False)
        pair_density = own_block[:, None] * lower_block[None, :]
        spectrum = jnp.fft.rfftn(pair_density, axes=(2, 3, 4))
        potential = jnp.fft.irfftn(spectrum * kernel, s=(NG, NG, NG), axes=(2, 3, 4)).astype(own_block.dtype)
        own_part = -jnp.sum(potential * lower_block[None, :], axis=1)
        lower_part = -jnp.sum(potential * own_block[:, None], axis=0)
        return own_part, lower_part

    own_parts, lower_parts = lax.map(group_step, jnp.arange(N_BAND, dtype=jnp.int32))
    result = own_parts + jnp.roll(lower_parts, -1, axis=0)
    return result.reshape(N_BAND * NBLK, NG, NG, NG)
```

```python
import functools
import math

import jax
import jax.numpy as jnp
import ml_dtypes
import numpy as np
from jax import lax
from jax.experimental import pallas as pl
from jax.experimental.pallas import tpu as pltpu
from jax.sharding import PartitionSpec as P

OMEGA = 0.5
N = 144
HALF = N // 2
GROUPS = 8
X = N // GROUPS
LANES = 128
TAIL = N - LANES
ROWS = X * 2 * X
SENT = ROWS + 8
POWER = 12.0
PLANE_GROUP = 6
PLANE_GROUPS = X // PLANE_GROUP
PACK = (PLANE_GROUP + 1) * N
BACK = PACK + 16
FORTH = (GROUPS, GROUPS)
BACKWARD = (GROUPS, GROUPS)
LATE = 5
F32 = jnp.float32
BF16 = jnp.bfloat16


def real_basis():
    freq = np.array([0] + [f for f in range(1, HALF) for _ in (0, 1)] + [HALF])
    points = np.arange(N)
    rows = []
    for idx, f in enumerate(freq):
        angle = 2.0 * np.pi * ((f * points) % N) / N
        if f in (0, HALF):
            rows.append(np.cos(angle) / np.sqrt(N))
        else:
            rows.append((np.cos(angle) if idx % 2 else np.sin(angle)) * np.sqrt(2.0 / N))
    return np.array(rows), freq


def z_order():
    return np.array(list(range(LANES)) + [N - 1] + list(range(LANES, N - 1)))


def main_mask():
    lane = np.arange(LANES)[None, :]
    row = np.arange(TAIL)[:, None]
    return lane < np.where(row == 0, 65, 63)


def column_freq_sq():
    freq = real_basis()[1]
    z_freq = freq[z_order()]
    sq = freq[:, None] ** 2 + z_freq[None, :LANES] ** 2
    turned = z_freq[LANES:, None] ** 2 + freq[LANES - 1 - np.arange(LANES)][None, :] ** 2
    sq[LANES:] = np.where(main_mask(), sq[LANES:], turned)
    return sq.astype(np.int32)


def split_const(values):
    high = values.astype(ml_dtypes.bfloat16)
    low = (values - high.astype(np.float64)).astype(ml_dtypes.bfloat16)
    return high, low


def stacked(values):
    return np.concatenate(split_const(values), axis=0)


@functools.cache
def tables():
    basis, freq = real_basis()
    z_basis = basis[z_order()]
    turned = np.zeros((N, LANES))
    turned[:, 63:] = basis[64::-1].T
    x_in, x_out = [], []
    for off in (0, 2, 4, 6):
        padded = np.zeros((N, GROUPS, 24))
        padded[:, :, off : off + X] = basis.reshape(N, GROUPS, X)
        padded = padded.reshape(N, GROUPS * 24)
        x_in.append(stacked(padded))
        x_out.append(stacked(padded.T))
    return {
        "yz": np.concatenate([stacked(z_basis.T), stacked(basis), stacked(np.pad(turned, ((0, 0), (0, TAIL))))]),
        "yz_t": np.concatenate([stacked(z_basis), stacked(basis.T), stacked(turned.T)]),
        "x": np.stack(x_in),
        "x_t": np.stack(x_out),
        "freq": freq.astype(np.int32),
        "column": column_freq_sq(),
    }


def coulomb(freq_sq):
    g_sq = freq_sq.astype(F32) * F32((2.0 * math.pi / N) ** 2)
    safe_sq = jnp.where(freq_sq > 0, g_sq, F32(1.0))
    values = jnp.where(
        freq_sq > 0,
        4.0 * math.pi / safe_sq * -jnp.expm1(-safe_sq / (4.0 * OMEGA * OMEGA)),
        F32(math.pi / (OMEGA * OMEGA)),
    )
    return jnp.where(freq_sq <= HALF**2, values, F32(0.0))


def mm(a, b):
    return lax.dot_general(a, b, (((1,), (0,)), ((), ())), preferred_element_type=F32)


def split(values):
    high = values.astype(BF16)
    return high, (values - high.astype(F32)).astype(BF16)


def right(values, table):
    rows = table.shape[0] // 2
    high, low = split(values)
    return mm(high, table[:rows]) + mm(high, table[rows:]) + mm(low, table[:rows])


def left(table, values):
    rows = table.shape[0] // 2
    high, low = split(values)
    both = mm(table, high)
    return both[:rows] + both[rows:] + mm(table[:rows], low)


def scale_of(largest):
    return jnp.floor(10.0 - jnp.log(jnp.maximum(largest, F32(2.0**-60))) * F32(1.0 / math.log(2.0)))


def encode(values, exponent):
    scaled = values * jnp.exp2(exponent)
    fourth = scaled * scaled
    fourth = fourth * fourth
    twelfth = fourth * fourth * fourth
    return jnp.where(values < 0, -twelfth, twelfth)


def decode(codes, exponent):
    size = jnp.exp2(jnp.log(jnp.abs(codes)) * F32(1.0 / math.log(2.0) / POWER) - exponent)
    return jnp.where(codes < 0, -size, size)


def partner(me, part, sign):
    return (me // 4 + part // 4) % 2 * 4 + (me % 4 + sign * (part % 4) + 4) % 4


def largest_of(values):
    return jnp.max(jnp.abs(values), axis=(0, 1), keepdims=True)


def store_parts(part_ref, out_refs, me_ref):
    starts = [part * ROWS for part in range(GROUPS)]
    if len(out_refs) > 1:
        starts = [pl.multiple_of(partner(me_ref[0], part, 1) * ROWS, 8) for part in range(GROUPS)]
    sizes = [
        jnp.max(jnp.abs(part_ref[pl.ds(start, ROWS), :]).reshape(ROWS // 8, 8, LANES), axis=0) for start in starts
    ]
    sizes = jnp.concatenate([jnp.max(values, axis=0, keepdims=True) for values in sizes], axis=0)
    exponents = scale_of(jnp.max(sizes, axis=1, keepdims=True))
    for part, start in enumerate(starts):
        exponent = exponents[part : part + 1]
        codes = encode(part_ref[pl.ds(start, ROWS), :], exponent)
        codes = jnp.concatenate([codes, jnp.broadcast_to(exponent, (8, LANES))], axis=0).astype(BF16)
        if len(out_refs) > 1:
            out_refs[part][...] = codes
        else:
            out_refs[0][part] = codes


def load_parts(in_refs, me_ref, part_ref):
    for part in range(GROUPS):
        if len(in_refs) > 1:
            codes, source = in_refs[part][...], partner(me_ref[0], part, -1)
        else:
            codes, source = in_refs[0][part], part
        codes = codes.astype(F32)
        start = pl.multiple_of(source * ROWS, 8) if len(in_refs) > 1 else source * ROWS
        part_ref[pl.ds(start, ROWS), :] = decode(codes[:ROWS], codes[ROWS : ROWS + 1])


def plane_of(pack_ref, group, slot):
    high = pack_ref[group, PLANE_GROUP * N : PACK, :].astype(F32)
    main = pack_ref[group, slot * N : (slot + 1) * N, :].astype(F32)
    return jnp.concatenate([main, high[:, slot * TAIL : (slot + 1) * TAIL]], axis=1)


def mask_rows():
    lane = lax.broadcasted_iota(jnp.int32, (TAIL, LANES), 1)
    row = lax.broadcasted_iota(jnp.int32, (TAIL, LANES), 0)
    return lane < jnp.where(row == 0, 65, 63)


def pack_kernel(band_ref, *refs):
    out_ref = refs[-1]
    tails = []
    for slot in range(PLANE_GROUP):
        values = band_ref[0, slot]
        out_ref[0, slot * N : (slot + 1) * N, :] = values[:, :LANES]
        tails.append(values[:, LANES:])
    tails.append(jnp.zeros((N, LANES - PLANE_GROUP * TAIL), BF16))
    out_ref[0, PLANE_GROUP * N : PACK, :] = jnp.concatenate(tails, axis=1)


def forward_kernel(groups, n_in, me_ref, own_ref, table_ref, *refs):
    low_ref, out_refs = refs[0], refs[1 + n_in :]
    out_refs, (part_ref, tail_ref) = out_refs[:-2], out_refs[-2:]
    z_table, y_table, turned_table = (table_ref[k * 2 * N : (k + 1) * 2 * N, :] for k in range(3))
    for pos, group in enumerate(groups):
        density = []
        for slot in range(PLANE_GROUP):
            lower = plane_of(low_ref, pos, slot)
            density += [own_ref[i, group * PLANE_GROUP + slot].astype(F32) * lower for i in (0, 1)]
        along_z = right(jnp.concatenate(density, axis=0), z_table)
        for slot in range(PLANE_GROUP):
            plane = group * PLANE_GROUP + slot
            pair = [along_z[(slot * 2 + i) * N : (slot * 2 + i + 1) * N] for i in (0, 1)]
            along_y = left(y_table, jnp.concatenate([values[:, :LANES] for values in pair], axis=1))
            for i in (0, 1):
                part_ref[pl.ds(i * X + plane, N, stride=2 * X), :] = along_y[:, i * LANES : (i + 1) * LANES]
                start = (plane * 2 + i) * TAIL
                tail_ref[start : start + TAIL, :] = pair[i][:, LANES:].T
    if not out_refs:
        return
    turned = right(tail_ref[...], turned_table[:, :LANES])
    mask = mask_rows()
    for plane in range(X):
        for i in (0, 1):
            rows = pl.ds(LANES * 2 * X + i * X + plane, TAIL, stride=2 * X)
            start = (plane * 2 + i) * TAIL
            part_ref[rows, :] = jnp.where(mask, part_ref[rows, :], turned[start : start + TAIL])
    store_parts(part_ref, out_refs, me_ref)


def filter_kernel(count, me_ref, kernel_ref, x_ref, x_t_ref, *refs):
    in_refs, out_refs, (part_ref, back_ref) = refs[:count], refs[count:-2], refs[-2:]
    load_parts(in_refs, me_ref, part_ref)
    units = [(m, m + 4) for base in range(0, 32, 8) for m in range(base, base + 4)]
    units += [(m,) for m in range(32, 36)]
    for unit in units:
        start = X * unit[0] % 8
        kind = start // 2
        columns = []
        for m in unit:
            first = X * m - start
            columns.append(
                jnp.concatenate([part_ref[g * ROWS + first : g * ROWS + first + 24, :] for g in range(GROUPS)], axis=0)
            )
        spectrum = left(x_ref[kind], jnp.concatenate(columns, axis=1))
        spectrum = spectrum * jnp.concatenate([kernel_ref[m // 2] for m in unit], axis=1)
        planes = left(x_t_ref[kind], spectrum)
        for pos, m in enumerate(unit):
            for g in range(GROUPS):
                back_ref[g * ROWS + X * m : g * ROWS + X * (m + 1), :] = planes[
                    g * 24 + start : g * 24 + start + X, pos * LANES : (pos + 1) * LANES
                ]
    store_parts(back_ref, out_refs, me_ref)


def inverse_kernel(groups, count, n_old, me_ref, own_ref, table_ref, *refs):
    refs = list(refs)

    def take(number):
        taken, refs[:number] = refs[:number], []
        return taken

    in_refs, low_refs, old_refs = take(count), take(PLANE_GROUPS if n_old == 0 else 1), take(n_old)
    sum_refs, (back_ref,), (*made, lower_ref) = take(2), take(1), refs
    part_ref, tail_ref = in_refs if count == 2 else made
    z_table, y_table = (table_ref[k * 2 * N : (k + 1) * 2 * N, :] for k in range(2))
    if count != 2:
        load_parts(in_refs, me_ref, part_ref)
        mask = mask_rows()
        high = []
        for plane in range(X):
            for i in (0, 1):
                rows = pl.ds(LANES * 2 * X + i * X + plane, TAIL, stride=2 * X)
                values = part_ref[rows, :]
                part_ref[rows, :] = jnp.where(mask, values, F32(0.0))
                high.append(jnp.where(mask, F32(0.0), values))
        tail_ref[...] = right(jnp.concatenate(high, axis=0), table_ref[4 * N : 4 * N + 2 * LANES, :])

    for pos, group in enumerate(groups):
        low_ref, in_pack = (low_refs[group], 0) if len(low_refs) > 1 else (low_refs[0], group)
        spectra = []
        for slot in range(PLANE_GROUP):
            plane = group * PLANE_GROUP + slot
            both = jnp.concatenate(
                [part_ref[pl.ds(i * X + plane, N, stride=2 * X), :] for i in (0, 1)], axis=1
            )
            along_y = left(y_table, both)
            for i in (0, 1):
                start = (plane * 2 + i) * TAIL
                spectra.append(
                    jnp.concatenate(
                        [along_y[:, i * LANES : (i + 1) * LANES], tail_ref[start : start + TAIL, :].T], axis=1
                    )
                )
        potential = right(jnp.concatenate(spectra, axis=0), z_table)
        largest = jnp.zeros((8, N), F32)
        for slot in range(PLANE_GROUP):
            plane = group * PLANE_GROUP + slot
            lower = plane_of(low_ref, in_pack, slot)
            given = jnp.zeros((N, N), F32)
            for i in (0, 1):
                mine = potential[(slot * 2 + i) * N : (slot * 2 + i + 1) * N]
                given = given - mine * own_ref[i, plane].astype(F32)
                if not old_refs:
                    sum_refs[i][pos * PLANE_GROUP + slot] = -(mine * lower)
                else:
                    sum_refs[i][pos * PLANE_GROUP + slot] = old_refs[i][plane] - mine * lower
            lower_ref[slot] = given
            largest = jnp.maximum(largest, jnp.max(jnp.abs(given).reshape(N // 8, 8, N), axis=0))
        exponent = scale_of(jnp.max(largest, axis=(0, 1), keepdims=True))
        tails = []
        for slot in range(PLANE_GROUP):
            given = lower_ref[slot]
            back_ref[pos, slot * N : (slot + 1) * N, :] = encode(given[:, :LANES], exponent).astype(BF16)
            tails.append(given[:, LANES:])
        tails.append(jnp.zeros((N, LANES - PLANE_GROUP * TAIL), F32))
        back_ref[pos, PLANE_GROUP * N : PACK, :] = encode(jnp.concatenate(tails, axis=1), exponent).astype(BF16)
        back_ref[pos, PACK:BACK, :] = jnp.broadcast_to(exponent, (16, LANES)).astype(BF16)


def add_kernel(count, n_back, *refs):
    sum_refs, back_refs, out_ref = refs[:count], refs[count : count + n_back], refs[-1]
    step = pl.program_id(0)

    def add(sum_ref, back_ref, group, half):
        exponent = back_ref[group, PACK:BACK, :].astype(F32)[:1, :1]
        high = decode(back_ref[group, PLANE_GROUP * N : PACK, :].astype(F32), exponent)
        for pos in range(PLANE_GROUP // 2):
            slot = half * (PLANE_GROUP // 2) + pos
            main = decode(back_ref[group, slot * N : (slot + 1) * N, :].astype(F32), exponent)
            given = jnp.concatenate([main, high[:, slot * TAIL : (slot + 1) * TAIL]], axis=1)
            out_ref[0, pos] = sum_ref[slot] + given

    for group in range(count):
        back = (back_refs[0], group) if n_back == 1 else (back_refs[group], 0)
        for half in (0, 1):
            pl.when(step == 2 * group + half)(functools.partial(add, sum_refs[group], *back, half))


def call(kernel, outs, scratch, rows, me, args, aliases=None):
    specs = [] if me is None else [pl.BlockSpec(memory_space=pltpu.SMEM)]
    me = () if me is None else (me,)
    return pl.pallas_call(
        kernel,
        out_shape=outs,
        in_specs=specs + [pl.BlockSpec(memory_space=pltpu.VMEM)] * len(args),
        scratch_shapes=scratch,
        input_output_aliases=aliases or {},
        compiler_params=pltpu.CompilerParams(vmem_limit_bytes=24 * 2**20),
        cost_estimate=pl.CostEstimate(flops=rows * 2**17, bytes_accessed=2**20, transcendentals=0),
    )(*me, *args)


def pack(orbitals, band, first, count, after):
    return pl.pallas_call(
        pack_kernel,
        out_shape=jax.ShapeDtypeStruct((count, PACK, LANES), BF16),
        grid=(count,),
        in_specs=[pl.BlockSpec((1, PLANE_GROUP, N, N), lambda g: (band, first + g, 0, 0))]
        + [pl.BlockSpec(memory_space=pl.ANY)] * len(after),
        out_specs=pl.BlockSpec((1, PACK, LANES), lambda g: (g, 0, 0)),
        compiler_params=pltpu.CompilerParams(vmem_limit_bytes=24 * 2**20),
        cost_estimate=pl.CostEstimate(flops=count * 2**28, bytes_accessed=2**20, transcendentals=0),
    )(orbitals, *after)


def add_back(band, first, sums, backs, out):
    vmem = pl.BlockSpec(memory_space=pltpu.VMEM)
    count, n_back = len(sums), len(backs)
    return pl.pallas_call(
        functools.partial(add_kernel, count, n_back),
        out_shape=jax.ShapeDtypeStruct((2, X, N, N), F32),
        grid=(2 * count,),
        in_specs=[vmem] * (count + n_back) + [pl.BlockSpec(memory_space=pl.ANY)] * len(out),
        out_specs=pl.BlockSpec((1, PLANE_GROUP // 2, N, N), lambda g: (band, 2 * first + g, 0, 0)),
        input_output_aliases={count + n_back: 0} if out else {},
        compiler_params=pltpu.CompilerParams(vmem_limit_bytes=24 * 2**20),
        cost_estimate=pl.CostEstimate(flops=count * 2**28, bytes_accessed=2**20, transcendentals=0),
    )(*sums, *backs, *out)


def shifted(value, axis, steps):
    count = lax.axis_size(axis)
    pairs = [(source, (source + steps) % count) for source in range(count)]
    return lax.ppermute(value, axis, pairs)


def exchange(parts):
    if len(parts) == 1:
        return [lax.all_to_all(parts[0], "grid", split_axis=0, concat_axis=0, tiled=True)]
    received = [parts[0]]
    for part in range(1, GROUPS):
        pairs = [(source, partner(source, part, 1)) for source in range(GROUPS)]
        received.append(lax.ppermute(parts[part], "grid", pairs))
    return received


def body(orbitals):
    table = {name: jnp.asarray(value) for name, value in tables().items()}
    rows = lax.dynamic_slice_in_dim(table["column"], lax.axis_index("grid") * X, X, axis=0)
    kernel = coulomb((table["freq"] ** 2)[None, :, None] + rows[:, None, :])

    back_shape = [jax.ShapeDtypeStruct((count, BACK, LANES), BF16) for count in (1, PLANE_GROUPS)]
    sent_shape = {1: [jax.ShapeDtypeStruct((GROUPS, SENT, LANES), BF16)]}
    sent_shape[GROUPS] = [jax.ShapeDtypeStruct((SENT, LANES), BF16)] * GROUPS
    part_shape = jax.ShapeDtypeStruct((GROUPS * ROWS, LANES), F32)
    tail_shape = jax.ShapeDtypeStruct((2 * X * TAIL, N), F32)
    planes_shape = jax.ShapeDtypeStruct((PLANE_GROUP, N, N), F32)
    sum_shape = jax.ShapeDtypeStruct((X, N, N), F32)
    part, tail, planes = (pltpu.VMEM(shape.shape, F32) for shape in (part_shape, tail_shape, planes_shape))
    me = lax.axis_index("grid").astype(jnp.int32).reshape(1)
    every = tuple(range(PLANE_GROUPS))

    packed, lower = [], []
    with jax.named_scope("pack"):
        for group in every:
            packed.append(pack(orbitals, 0, group, 1, packed[-1:]))
            lower.append(shifted(packed[-1], "band", 1))
    with jax.named_scope("forward"):
        made = []
        for group in every[:-1]:
            made = call(
                functools.partial(forward_kernel, (group,), len(made)), [part_shape, tail_shape], [], 20000, me,
                [orbitals, table["yz"], lower[group], *made], {4: 0, 5: 1} if made else {},
            )
            if group == 0:
                moved = shifted(pack(orbitals, 1, 0, PLANE_GROUPS, made[1:]), "band", 1)
        *first_forth, _, _ = call(
            functools.partial(forward_kernel, every[-1:], 2), [*sent_shape[FORTH[0]], part_shape, tail_shape], [],
            20000, me, [orbitals, table["yz"], lower[-1], *made], {4: FORTH[0], 5: FORTH[0] + 1},
        )
        second_forth = call(
            functools.partial(forward_kernel, every, 0), sent_shape[FORTH[1]], [part, tail], 60000, me,
            [orbitals, table["yz"], moved],
        )
    spectra = [list(lax.optimization_barrier((exchange(first_forth), list(second_forth)))[0])]
    filtered = []
    for j in (0, 1):
        with jax.named_scope("filter"):
            sent = call(
                functools.partial(filter_kernel, FORTH[j]), sent_shape[BACKWARD[j]], [part, part], 60000, me,
                [kernel, table["x"], table["x_t"], *spectra[j]],
            )
            if j == 0:
                late = lax.optimization_barrier((list(second_forth[LATE:]), list(sent)))[0]
                spectra.append(exchange([*second_forth[:LATE], *late]))
            filtered.append(exchange(sent))
    with jax.named_scope("inverse"):
        *older, first_back = call(
            functools.partial(inverse_kernel, every, BACKWARD[0], 0), [sum_shape] * 2 + [back_shape[1]],
            [part, tail, planes], 60000, me, [orbitals, table["yz_t"], *filtered[0], *lower],
        )
        first_back = shifted(first_back, "band", -1)
        sums, second_back = [], []
        for group in every:
            shapes = [planes_shape] * 2 + [back_shape[0]]
            if group == 0:
                *results, part_out, tail_out = call(
                    functools.partial(inverse_kernel, (group,), BACKWARD[1], 2), [*shapes, part_shape, tail_shape],
                    [planes], 30000, me, [orbitals, table["yz_t"], *filtered[1], moved, *older],
                )
            else:
                results = call(
                    functools.partial(inverse_kernel, (group,), 2, 2), shapes, [planes], 20000, me,
                    [orbitals, table["yz_t"], part_out, tail_out, moved, *older],
                )
            sums.append(results[:2])
            second_back.append(shifted(results[2], "band", -1))
    with jax.named_scope("add"):
        out = add_back(0, 0, [pair[0] for pair in sums], [first_back], [])
        out = add_back(1, 0, [pair[1] for pair in sums[:-1]], second_back[:-1], [out])
        return add_back(1, PLANE_GROUPS - 1, [sums[-1][1]], second_back[-1:], [out])


def solution(mesh):
    in_specs = (P("band", "grid", None, None),)
    out_specs = P("band", "grid", None, None)
    return jax.shard_map(body, mesh=mesh, in_specs=in_specs, out_specs=out_specs, check_vma=False)
```

```python
import functools
import math

import jax
import jax.numpy as jnp
import ml_dtypes
import numpy as np
from jax import lax
from jax.experimental import pallas as pl
from jax.experimental.pallas import tpu as pltpu
from jax.sharding import PartitionSpec as P

OMEGA = 0.5
N = 144
HALF = N // 2
GROUPS = 8
X = N // GROUPS
LANES = 128
TAIL = N - LANES
ROWS = X * 2 * X
SENT = ROWS + 8
POWER = 12.0
PLANE_GROUP = 6
PLANE_GROUPS = X // PLANE_GROUP
PACK = (PLANE_GROUP + 1) * N
BACK = PACK + 16
FORTH = (GROUPS, GROUPS)
BACKWARD = (GROUPS, GROUPS)
LATE = 5
F32 = jnp.float32
BF16 = jnp.bfloat16


def real_basis():
    freq = np.array([0] + [f for f in range(1, HALF) for _ in (0, 1)] + [HALF])
    points = np.arange(N)
    rows = []
    for idx, f in enumerate(freq):
        angle = 2.0 * np.pi * ((f * points) % N) / N
        if f in (0, HALF):
            rows.append(np.cos(angle) / np.sqrt(N))
        else:
            rows.append((np.cos(angle) if idx % 2 else np.sin(angle)) * np.sqrt(2.0 / N))
    return np.array(rows), freq


def z_order():
    return np.array(list(range(LANES)) + [N - 1] + list(range(LANES, N - 1)))


def main_mask():
    lane = np.arange(LANES)[None, :]
    row = np.arange(TAIL)[:, None]
    return lane < np.where(row == 0, 65, 63)


def column_freq_sq():
    freq = real_basis()[1]
    z_freq = freq[z_order()]
    sq = freq[:, None] ** 2 + z_freq[None, :LANES] ** 2
    turned = z_freq[LANES:, None] ** 2 + freq[LANES - 1 - np.arange(LANES)][None, :] ** 2
    sq[LANES:] = np.where(main_mask(), sq[LANES:], turned)
    return sq.astype(np.int32)


def split_const(values):
    high = values.astype(ml_dtypes.bfloat16)
    low = (values - high.astype(np.float64)).astype(ml_dtypes.bfloat16)
    return high, low


def stacked(values):
    return np.concatenate(split_const(values), axis=0)


@functools.cache
def tables():
    basis, freq = real_basis()
    z_basis = basis[z_order()]
    turned = np.zeros((N, LANES))
    turned[:, 63:] = basis[64::-1].T
    x_in, x_out = [], []
    for off in (0, 2, 4, 6):
        padded = np.zeros((N, GROUPS, 24))
        padded[:, :, off : off + X] = basis.reshape(N, GROUPS, X)
        padded = padded.reshape(N, GROUPS * 24)
        x_in.append(stacked(padded))
        x_out.append(stacked(padded.T))
    return {
        "yz": np.concatenate([stacked(z_basis.T), stacked(basis), stacked(np.pad(turned, ((0, 0), (0, TAIL))))]),
        "yz_t": np.concatenate([stacked(z_basis), stacked(basis.T), stacked(turned.T)]),
        "x": np.stack(x_in),
        "x_t": np.stack(x_out),
        "freq": freq.astype(np.int32),
        "column": column_freq_sq(),
    }


def coulomb(freq_sq):
    g_sq = freq_sq.astype(F32) * F32((2.0 * math.pi / N) ** 2)
    safe_sq = jnp.where(freq_sq > 0, g_sq, F32(1.0))
    values = jnp.where(
        freq_sq > 0,
        4.0 * math.pi / safe_sq * -jnp.expm1(-safe_sq / (4.0 * OMEGA * OMEGA)),
        F32(math.pi / (OMEGA * OMEGA)),
    )
    return jnp.where(freq_sq <= HALF**2, values, F32(0.0))


def mm(a, b):
    return lax.dot_general(a, b, (((1,), (0,)), ((), ())), preferred_element_type=F32)


def split(values):
    high = values.astype(BF16)
    return high, (values - high.astype(F32)).astype(BF16)


def right(values, table):
    rows = table.shape[0] // 2
    high, low = split(values)
    if rows == LANES:
        return mm(high, table[:rows]) + mm(high, table[rows:]) + mm(low, table[:rows])
    first = mm(
        jnp.concatenate([high[:, :LANES], low[:, :LANES]], axis=1),
        jnp.concatenate([table[:LANES], table[:LANES]], axis=0),
    )
    second = jnp.concatenate([high, low[:, LANES:], high[:, LANES:]], axis=1)
    return first + mm(
        second,
        jnp.concatenate([table[rows : rows + LANES], table[LANES:rows], table[LANES:rows], table[rows + LANES :]], axis=0),
    )


def left(table, values):
    rows = table.shape[0] // 2
    high, low = split(values)
    both = mm(table, high)
    return both[:rows] + both[rows:] + mm(table[:rows], low)


def scale_of(largest):
    return jnp.floor(10.0 - jnp.log(jnp.maximum(largest, F32(2.0**-60))) * F32(1.0 / math.log(2.0)))


def encode(values, exponent):
    scaled = values * jnp.exp2(exponent)
    fourth = scaled * scaled
    fourth = fourth * fourth
    twelfth = fourth * fourth * fourth
    return jnp.where(values < 0, -twelfth, twelfth)


def decode(codes, exponent):
    size = jnp.exp2(jnp.log(jnp.abs(codes)) * F32(1.0 / math.log(2.0) / POWER) - exponent)
    return jnp.where(codes < 0, -size, size)


def partner(me, part, sign):
    return (me // 4 + part // 4) % 2 * 4 + (me % 4 + sign * (part % 4) + 4) % 4


def largest_of(values):
    return jnp.max(jnp.abs(values), axis=(0, 1), keepdims=True)


def store_parts(part_ref, out_refs, me_ref):
    starts = [part * ROWS for part in range(GROUPS)]
    if len(out_refs) > 1:
        starts = [pl.multiple_of(partner(me_ref[0], part, 1) * ROWS, 8) for part in range(GROUPS)]
    sizes = [
        jnp.max(jnp.abs(part_ref[pl.ds(start, ROWS), :]).reshape(ROWS // 8, 8, LANES), axis=0) for start in starts
    ]
    sizes = jnp.concatenate([jnp.max(values, axis=0, keepdims=True) for values in sizes], axis=0)
    exponents = scale_of(jnp.max(sizes, axis=1, keepdims=True))
    for part, start in enumerate(starts):
        exponent = exponents[part : part + 1]
        codes = encode(part_ref[pl.ds(start, ROWS), :], exponent)
        codes = jnp.concatenate([codes, jnp.broadcast_to(exponent, (8, LANES))], axis=0).astype(BF16)
        if len(out_refs) > 1:
            out_refs[part][...] = codes
        else:
            out_refs[0][part] = codes


def load_parts(in_refs, me_ref, part_ref):
    for part in range(GROUPS):
        if len(in_refs) > 1:
            codes, source = in_refs[part][...], partner(me_ref[0], part, -1)
        else:
            codes, source = in_refs[0][part], part
        codes = codes.astype(F32)
        start = pl.multiple_of(source * ROWS, 8) if len(in_refs) > 1 else source * ROWS
        part_ref[pl.ds(start, ROWS), :] = decode(codes[:ROWS], codes[ROWS : ROWS + 1])


def plane_of(pack_ref, group, slot):
    high = pack_ref[group, PLANE_GROUP * N : PACK, :].astype(F32)
    main = pack_ref[group, slot * N : (slot + 1) * N, :].astype(F32)
    return jnp.concatenate([main, high[:, slot * TAIL : (slot + 1) * TAIL]], axis=1)


def mask_rows():
    lane = lax.broadcasted_iota(jnp.int32, (TAIL, LANES), 1)
    row = lax.broadcasted_iota(jnp.int32, (TAIL, LANES), 0)
    return lane < jnp.where(row == 0, 65, 63)


def pack_kernel(band_ref, *refs):
    out_ref = refs[-1]
    tails = []
    for slot in range(PLANE_GROUP):
        values = band_ref[0, slot]
        out_ref[0, slot * N : (slot + 1) * N, :] = values[:, :LANES]
        tails.append(values[:, LANES:])
    tails.append(jnp.zeros((N, LANES - PLANE_GROUP * TAIL), BF16))
    out_ref[0, PLANE_GROUP * N : PACK, :] = jnp.concatenate(tails, axis=1)


def forward_kernel(groups, n_in, me_ref, own_ref, table_ref, *refs):
    low_ref, out_refs = refs[0], refs[1 + n_in :]
    out_refs, (part_ref, tail_ref) = out_refs[:-2], out_refs[-2:]
    z_table, y_table, turned_table = (table_ref[k * 2 * N : (k + 1) * 2 * N, :] for k in range(3))
    for pos, group in enumerate(groups):
        density = []
        for slot in range(PLANE_GROUP):
            lower = plane_of(low_ref, pos, slot)
            density += [own_ref[i, group * PLANE_GROUP + slot].astype(F32) * lower for i in (0, 1)]
        along_z = right(jnp.concatenate(density, axis=0), z_table)
        for slot in range(PLANE_GROUP):
            plane = group * PLANE_GROUP + slot
            pair = [along_z[(slot * 2 + i) * N : (slot * 2 + i + 1) * N] for i in (0, 1)]
            along_y = left(y_table, jnp.concatenate([values[:, :LANES] for values in pair], axis=1))
            for i in (0, 1):
                part_ref[pl.ds(i * X + plane, N, stride=2 * X), :] = along_y[:, i * LANES : (i + 1) * LANES]
                start = (plane * 2 + i) * TAIL
                tail_ref[start : start + TAIL, :] = pair[i][:, LANES:].T
    if not out_refs:
        return
    turned = right(tail_ref[...], turned_table[:, :LANES])
    mask = mask_rows()
    for plane in range(X):
        for i in (0, 1):
            rows = pl.ds(LANES * 2 * X + i * X + plane, TAIL, stride=2 * X)
            start = (plane * 2 + i) * TAIL
            part_ref[rows, :] = jnp.where(mask, part_ref[rows, :], turned[start : start + TAIL])
    store_parts(part_ref, out_refs, me_ref)


def filter_kernel(count, me_ref, kernel_ref, x_ref, x_t_ref, *refs):
    in_refs, out_refs, (part_ref, back_ref) = refs[:count], refs[count:-2], refs[-2:]
    load_parts(in_refs, me_ref, part_ref)
    units = [tuple(range(kind, 2 * X, 4)) for kind in range(4)]
    for unit in units:
        start = X * unit[0] % 8
        kind = start // 2
        columns = []
        for m in unit:
            first = X * m - start
            columns.append(
                jnp.concatenate([part_ref[g * ROWS + first : g * ROWS + first + 24, :] for g in range(GROUPS)], axis=0)
            )
        spectrum = left(x_ref[kind], jnp.concatenate(columns, axis=1))
        spectrum = spectrum * jnp.concatenate([kernel_ref[m // 2] for m in unit], axis=1)
        planes = left(x_t_ref[kind], spectrum)
        for pos, m in enumerate(unit):
            for g in range(GROUPS):
                back_ref[g * ROWS + X * m : g * ROWS + X * (m + 1), :] = planes[
                    g * 24 + start : g * 24 + start + X, pos * LANES : (pos + 1) * LANES
                ]
    store_parts(back_ref, out_refs, me_ref)


def inverse_kernel(groups, count, n_old, me_ref, own_ref, table_ref, *refs):
    refs = list(refs)

    def take(number):
        taken, refs[:number] = refs[:number], []
        return taken

    in_refs, low_refs, old_refs = take(count), take(PLANE_GROUPS if n_old == 0 else 1), take(n_old)
    sum_refs, (back_ref,), (*made, lower_ref) = take(2), take(1), refs
    part_ref, tail_ref = in_refs if count == 2 else made
    z_table, y_table = (table_ref[k * 2 * N : (k + 1) * 2 * N, :] for k in range(2))
    if count != 2:
        load_parts(in_refs, me_ref, part_ref)
        mask = mask_rows()
        high = []
        for plane in range(X):
            for i in (0, 1):
                rows = pl.ds(LANES * 2 * X + i * X + plane, TAIL, stride=2 * X)
                values = part_ref[rows, :]
                part_ref[rows, :] = jnp.where(mask, values, F32(0.0))
                high.append(jnp.where(mask, F32(0.0), values))
        tail_ref[...] = right(jnp.concatenate(high, axis=0), table_ref[4 * N : 4 * N + 2 * LANES, :])

    for pos, group in enumerate(groups):
        low_ref, in_pack = (low_refs[group], 0) if len(low_refs) > 1 else (low_refs[0], group)
        spectra, tails = [], []
        for slot in range(PLANE_GROUP):
            plane = group * PLANE_GROUP + slot
            both = jnp.concatenate(
                [part_ref[pl.ds(i * X + plane, N, stride=2 * X), :] for i in (0, 1)], axis=1
            )
            along_y = left(y_table, both)
            for i in (0, 1):
                start = (plane * 2 + i) * TAIL
                spectra.append(along_y[:, i * LANES : (i + 1) * LANES])
                tails.append(tail_ref[start : start + TAIL, :].T)
        high, low = split(jnp.concatenate(spectra, axis=0))
        tail_high, tail_low = split(jnp.concatenate(tails, axis=0))
        first = mm(jnp.concatenate([high, low], axis=1), jnp.concatenate([z_table[:LANES]] * 2, axis=0))
        second = jnp.concatenate([high, tail_high, tail_low, tail_high], axis=1)
        rest = [z_table[N : N + LANES], z_table[LANES:N], z_table[LANES:N], z_table[N + LANES :]]
        potential = first + mm(second, jnp.concatenate(rest, axis=0))
        largest = jnp.zeros((8, N), F32)
        for slot in range(PLANE_GROUP):
            plane = group * PLANE_GROUP + slot
            lower = plane_of(low_ref, in_pack, slot)
            given = jnp.zeros((N, N), F32)
            for i in (0, 1):
                mine = potential[(slot * 2 + i) * N : (slot * 2 + i + 1) * N]
                given = given - mine * own_ref[i, plane].astype(F32)
                if not old_refs:
                    sum_refs[i][pos * PLANE_GROUP + slot] = -(mine * lower)
                else:
                    sum_refs[i][pos * PLANE_GROUP + slot] = old_refs[i][plane] - mine * lower
            lower_ref[slot] = given
            largest = jnp.maximum(largest, jnp.max(jnp.abs(given).reshape(N // 8, 8, N), axis=0))
        exponent = scale_of(jnp.max(largest, axis=(0, 1), keepdims=True))
        tails = []
        for slot in range(PLANE_GROUP):
            given = lower_ref[slot]
            back_ref[pos, slot * N : (slot + 1) * N, :] = encode(given[:, :LANES], exponent).astype(BF16)
            tails.append(given[:, LANES:])
        tails.append(jnp.zeros((N, LANES - PLANE_GROUP * TAIL), F32))
        back_ref[pos, PLANE_GROUP * N : PACK, :] = encode(jnp.concatenate(tails, axis=1), exponent).astype(BF16)
        back_ref[pos, PACK:BACK, :] = jnp.broadcast_to(exponent, (16, LANES)).astype(BF16)


def add_kernel(count, n_back, *refs):
    sum_refs, back_refs, out_ref = refs[:count], refs[count : count + n_back], refs[-1]
    step = pl.program_id(0)

    def add(sum_ref, back_ref, group):
        exponent = back_ref[group, PACK:BACK, :].astype(F32)[:1, :1]
        high = decode(back_ref[group, PLANE_GROUP * N : PACK, :].astype(F32), exponent)
        for slot in range(PLANE_GROUP):
            main = decode(back_ref[group, slot * N : (slot + 1) * N, :].astype(F32), exponent)
            given = jnp.concatenate([main, high[:, slot * TAIL : (slot + 1) * TAIL]], axis=1)
            out_ref[0, slot] = sum_ref[slot] + given

    for group in range(count):
        back = (back_refs[0], group) if n_back == 1 else (back_refs[group], 0)
        pl.when(step == group)(functools.partial(add, sum_refs[group], *back))


def call(kernel, outs, scratch, rows, me, args, aliases=None):
    specs = [] if me is None else [pl.BlockSpec(memory_space=pltpu.SMEM)]
    me = () if me is None else (me,)
    return pl.pallas_call(
        kernel,
        out_shape=outs,
        in_specs=specs + [pl.BlockSpec(memory_space=pltpu.VMEM)] * len(args),
        scratch_shapes=scratch,
        input_output_aliases=aliases or {},
        compiler_params=pltpu.CompilerParams(vmem_limit_bytes=24 * 2**20),
        cost_estimate=pl.CostEstimate(flops=rows * 2**17, bytes_accessed=2**20, transcendentals=0),
    )(*me, *args)


def pack(orbitals, band, first, count, after):
    return pl.pallas_call(
        pack_kernel,
        out_shape=jax.ShapeDtypeStruct((count, PACK, LANES), BF16),
        grid=(count,),
        in_specs=[pl.BlockSpec((1, PLANE_GROUP, N, N), lambda g: (band, first + g, 0, 0))]
        + [pl.BlockSpec(memory_space=pl.ANY)] * len(after),
        out_specs=pl.BlockSpec((1, PACK, LANES), lambda g: (g, 0, 0)),
        compiler_params=pltpu.CompilerParams(vmem_limit_bytes=24 * 2**20),
        cost_estimate=pl.CostEstimate(flops=count * 2**28, bytes_accessed=2**20, transcendentals=0),
    )(orbitals, *after)


def add_back(band, first, sums, backs, out):
    vmem = pl.BlockSpec(memory_space=pltpu.VMEM)
    count, n_back = len(sums), len(backs)
    return pl.pallas_call(
        functools.partial(add_kernel, count, n_back),
        out_shape=jax.ShapeDtypeStruct((2, X, N, N), F32),
        grid=(count,),
        in_specs=[vmem] * (count + n_back) + [pl.BlockSpec(memory_space=pl.ANY)] * len(out),
        out_specs=pl.BlockSpec((1, PLANE_GROUP, N, N), lambda g: (band, first + g, 0, 0)),
        input_output_aliases={count + n_back: 0} if out else {},
        compiler_params=pltpu.CompilerParams(vmem_limit_bytes=24 * 2**20),
        cost_estimate=pl.CostEstimate(flops=count * 2**28, bytes_accessed=2**20, transcendentals=0),
    )(*sums, *backs, *out)


def shifted(value, axis, steps):
    count = lax.axis_size(axis)
    pairs = [(source, (source + steps) % count) for source in range(count)]
    return lax.ppermute(value, axis, pairs)


def exchange(parts):
    if len(parts) == 1:
        return [lax.all_to_all(parts[0], "grid", split_axis=0, concat_axis=0, tiled=True)]
    received = [parts[0]]
    for part in range(1, GROUPS):
        pairs = [(source, partner(source, part, 1)) for source in range(GROUPS)]
        received.append(lax.ppermute(parts[part], "grid", pairs))
    return received


def body(orbitals):
    table = {name: jnp.asarray(value) for name, value in tables().items()}
    rows = lax.dynamic_slice_in_dim(table["column"], lax.axis_index("grid") * X, X, axis=0)
    kernel = coulomb((table["freq"] ** 2)[None, :, None] + rows[:, None, :])

    back_shape = [jax.ShapeDtypeStruct((count, BACK, LANES), BF16) for count in (1, PLANE_GROUPS)]
    sent_shape = {1: [jax.ShapeDtypeStruct((GROUPS, SENT, LANES), BF16)]}
    sent_shape[GROUPS] = [jax.ShapeDtypeStruct((SENT, LANES), BF16)] * GROUPS
    part_shape = jax.ShapeDtypeStruct((GROUPS * ROWS, LANES), F32)
    tail_shape = jax.ShapeDtypeStruct((2 * X * TAIL, N), F32)
    planes_shape = jax.ShapeDtypeStruct((PLANE_GROUP, N, N), F32)
    sum_shape = jax.ShapeDtypeStruct((X, N, N), F32)
    part, tail, planes = (pltpu.VMEM(shape.shape, F32) for shape in (part_shape, tail_shape, planes_shape))
    me = lax.axis_index("grid").astype(jnp.int32).reshape(1)
    every = tuple(range(PLANE_GROUPS))

    packed, lower = [], []
    with jax.named_scope("pack"):
        for group in every:
            packed.append(pack(orbitals, 0, group, 1, packed[-1:]))
            lower.append(shifted(packed[-1], "band", 1))
    with jax.named_scope("forward"):
        made = []
        for group in every[:-1]:
            made = call(
                functools.partial(forward_kernel, (group,), len(made)), [part_shape, tail_shape], [], 20000, me,
                [orbitals, table["yz"], lower[group], *made], {4: 0, 5: 1} if made else {},
            )
            if group == 0:
                moved = shifted(pack(orbitals, 1, 0, PLANE_GROUPS, made[1:]), "band", 1)
        *first_forth, _, _ = call(
            functools.partial(forward_kernel, every[-1:], 2), [*sent_shape[FORTH[0]], part_shape, tail_shape], [],
            20000, me, [orbitals, table["yz"], lower[-1], *made], {4: FORTH[0], 5: FORTH[0] + 1},
        )
        second_forth = call(
            functools.partial(forward_kernel, every, 0), sent_shape[FORTH[1]], [part, tail], 60000, me,
            [orbitals, table["yz"], moved],
        )
    spectra = [list(lax.optimization_barrier((exchange(first_forth), list(second_forth)))[0])]
    filtered = []
    for j in (0, 1):
        with jax.named_scope("filter"):
            sent = call(
                functools.partial(filter_kernel, FORTH[j]), sent_shape[BACKWARD[j]], [part, part], 60000, me,
                [kernel, table["x"], table["x_t"], *spectra[j]],
            )
            if j == 0:
                late = lax.optimization_barrier((list(second_forth[LATE:]), list(sent)))[0]
                spectra.append(exchange([*second_forth[:LATE], *late]))
            filtered.append(exchange(sent))
    with jax.named_scope("inverse"):
        *older, first_back = call(
            functools.partial(inverse_kernel, every, BACKWARD[0], 0), [sum_shape] * 2 + [back_shape[1]],
            [part, tail, planes], 60000, me, [orbitals, table["yz_t"], *filtered[0], *lower],
        )
        first_back = shifted(first_back, "band", -1)
        sums, second_back = [], []
        for group in every:
            shapes = [planes_shape] * 2 + [back_shape[0]]
            if group == 0:
                *results, part_out, tail_out = call(
                    functools.partial(inverse_kernel, (group,), BACKWARD[1], 2), [*shapes, part_shape, tail_shape],
                    [planes], 30000, me, [orbitals, table["yz_t"], *filtered[1], moved, *older],
                )
            else:
                results = call(
                    functools.partial(inverse_kernel, (group,), 2, 2), shapes, [planes], 20000, me,
                    [orbitals, table["yz_t"], part_out, tail_out, moved, *older],
                )
            sums.append(results[:2])
            second_back.append(shifted(results[2], "band", -1))
    with jax.named_scope("add"):
        out = add_back(0, 0, [pair[0] for pair in sums], [first_back], [])
        out = add_back(1, 0, [pair[1] for pair in sums[:-1]], second_back[:-1], [out])
        return add_back(1, PLANE_GROUPS - 1, [sums[-1][1]], second_back[-1:], [out])


def solution(mesh):
    in_specs = (P("band", "grid", None, None),)
    out_specs = P("band", "grid", None, None)
    return jax.shard_map(body, mesh=mesh, in_specs=in_specs, out_specs=out_specs, check_vma=False)
```

```python
import functools
import math

import jax
import jax.numpy as jnp
import ml_dtypes
import numpy as np
from jax import lax
from jax.experimental import pallas as pl
from jax.experimental.pallas import tpu as pltpu
from jax.sharding import PartitionSpec as P

OMEGA = 0.5
N = 144
HALF = N // 2
GROUPS = 8
X = N // GROUPS
LANES = 128
TAIL = N - LANES
ROWS = X * 2 * X
SENT = ROWS + 8
POWER = 12.0
PLANE_GROUP = 6
PLANE_GROUPS = X // PLANE_GROUP
PACK = (PLANE_GROUP + 1) * N
BACK = PACK + 16
FORTH = (GROUPS, GROUPS)
BACKWARD = (GROUPS, GROUPS)
LATE = 5
F32 = jnp.float32
BF16 = jnp.bfloat16


def real_basis():
    freq = np.array([0] + [f for f in range(1, HALF) for _ in (0, 1)] + [HALF])
    points = np.arange(N)
    rows = []
    for idx, f in enumerate(freq):
        angle = 2.0 * np.pi * ((f * points) % N) / N
        if f in (0, HALF):
            rows.append(np.cos(angle) / np.sqrt(N))
        else:
            rows.append((np.cos(angle) if idx % 2 else np.sin(angle)) * np.sqrt(2.0 / N))
    return np.array(rows), freq


def z_order():
    return np.array(list(range(LANES)) + [N - 1] + list(range(LANES, N - 1)))


def main_mask():
    lane = np.arange(LANES)[None, :]
    row = np.arange(TAIL)[:, None]
    return lane < np.where(row == 0, 65, 63)


def column_freq_sq():
    freq = real_basis()[1]
    z_freq = freq[z_order()]
    sq = freq[:, None] ** 2 + z_freq[None, :LANES] ** 2
    turned = z_freq[LANES:, None] ** 2 + freq[LANES - 1 - np.arange(LANES)][None, :] ** 2
    sq[LANES:] = np.where(main_mask(), sq[LANES:], turned)
    return sq.astype(np.int32)


def split_const(values):
    high = values.astype(ml_dtypes.bfloat16)
    low = (values - high.astype(np.float64)).astype(ml_dtypes.bfloat16)
    return high, low


def stacked(values):
    return np.concatenate(split_const(values), axis=0)


@functools.cache
def tables():
    basis, freq = real_basis()
    z_basis = basis[z_order()]
    turned = np.zeros((N, LANES))
    turned[:, 63:] = basis[64::-1].T
    x_in, x_out = [], []
    for off in (0, 2, 4, 6):
        padded = np.zeros((N, GROUPS, 24))
        padded[:, :, off : off + X] = basis.reshape(N, GROUPS, X)
        padded = padded.reshape(N, GROUPS * 24)
        x_in.append(stacked(padded))
        x_out.append(stacked(padded.T))
    return {
        "yz": np.concatenate([stacked(z_basis.T), stacked(basis), stacked(np.pad(turned, ((0, 0), (0, TAIL))))]),
        "yz_t": np.concatenate([stacked(z_basis), stacked(basis.T), stacked(turned.T)]),
        "x": np.stack(x_in),
        "x_t": np.stack(x_out),
        "freq": freq.astype(np.int32),
        "column": column_freq_sq(),
    }


def coulomb(freq_sq):
    g_sq = freq_sq.astype(F32) * F32((2.0 * math.pi / N) ** 2)
    safe_sq = jnp.where(freq_sq > 0, g_sq, F32(1.0))
    values = jnp.where(
        freq_sq > 0,
        4.0 * math.pi / safe_sq * -jnp.expm1(-safe_sq / (4.0 * OMEGA * OMEGA)),
        F32(math.pi / (OMEGA * OMEGA)),
    )
    return jnp.where(freq_sq <= HALF**2, values, F32(0.0))


def mm(a, b):
    return lax.dot_general(a, b, (((1,), (0,)), ((), ())), preferred_element_type=F32)


def split(values):
    high = values.astype(BF16)
    return high, (values - high.astype(F32)).astype(BF16)


def right(values, table):
    rows = table.shape[0] // 2
    high, low = split(values)
    if rows == LANES:
        return mm(high, table[:rows]) + mm(high, table[rows:]) + mm(low, table[:rows])
    first = mm(
        jnp.concatenate([high[:, :LANES], low[:, :LANES]], axis=1),
        jnp.concatenate([table[:LANES], table[:LANES]], axis=0),
    )
    second = jnp.concatenate([high, low[:, LANES:], high[:, LANES:]], axis=1)
    return first + mm(
        second,
        jnp.concatenate([table[rows : rows + LANES], table[LANES:rows], table[LANES:rows], table[rows + LANES :]], axis=0),
    )


def left(table, values):
    rows = table.shape[0] // 2
    high, low = split(values)
    both = mm(table, high)
    return both[:rows] + both[rows:] + mm(table[:rows], low)


def scale_of(largest):
    return jnp.floor(10.0 - jnp.log(jnp.maximum(largest, F32(2.0**-60))) * F32(1.0 / math.log(2.0)))


def encode(values, exponent):
    scaled = values * jnp.exp2(exponent)
    fourth = scaled * scaled
    fourth = fourth * fourth
    twelfth = fourth * fourth * fourth
    return jnp.where(values < 0, -twelfth, twelfth)


def decode(codes, exponent):
    size = jnp.exp2(jnp.log(jnp.abs(codes)) * F32(1.0 / math.log(2.0) / POWER) - exponent)
    return jnp.where(codes < 0, -size, size)


def partner(me, part, sign):
    return (me // 4 + part // 4) % 2 * 4 + (me % 4 + sign * (part % 4) + 4) % 4


def largest_of(values):
    return jnp.max(jnp.abs(values), axis=(0, 1), keepdims=True)


def store_parts(part_ref, out_refs, me_ref):
    starts = [part * ROWS for part in range(GROUPS)]
    if len(out_refs) > 1:
        starts = [pl.multiple_of(partner(me_ref[0], part, 1) * ROWS, 8) for part in range(GROUPS)]
    sizes = [
        jnp.max(jnp.abs(part_ref[pl.ds(start, ROWS), :]).reshape(ROWS // 8, 8, LANES), axis=0) for start in starts
    ]
    sizes = jnp.concatenate([jnp.max(values, axis=0, keepdims=True) for values in sizes], axis=0)
    exponents = scale_of(jnp.max(sizes, axis=1, keepdims=True))
    for part, start in enumerate(starts):
        exponent = exponents[part : part + 1]
        codes = encode(part_ref[pl.ds(start, ROWS), :], exponent)
        codes = jnp.concatenate([codes, jnp.broadcast_to(exponent, (8, LANES))], axis=0).astype(BF16)
        if len(out_refs) > 1:
            out_refs[part][...] = codes
        else:
            out_refs[0][part] = codes


def load_parts(in_refs, me_ref, part_ref):
    for part in range(GROUPS):
        if len(in_refs) > 1:
            codes, source = in_refs[part][...], partner(me_ref[0], part, -1)
        else:
            codes, source = in_refs[0][part], part
        codes = codes.astype(F32)
        start = pl.multiple_of(source * ROWS, 8) if len(in_refs) > 1 else source * ROWS
        part_ref[pl.ds(start, ROWS), :] = decode(codes[:ROWS], codes[ROWS : ROWS + 1])


def plane_of(pack_ref, group, slot):
    high = pack_ref[group, PLANE_GROUP * N : PACK, :].astype(F32)
    main = pack_ref[group, slot * N : (slot + 1) * N, :].astype(F32)
    return jnp.concatenate([main, high[:, slot * TAIL : (slot + 1) * TAIL]], axis=1)


def mask_rows():
    lane = lax.broadcasted_iota(jnp.int32, (TAIL, LANES), 1)
    row = lax.broadcasted_iota(jnp.int32, (TAIL, LANES), 0)
    return lane < jnp.where(row == 0, 65, 63)


def pack_kernel(band, first, band_ref, *refs):
    out_ref, planes_ref, sem = refs[-3:]
    start = (first + pl.program_id(0)) * PLANE_GROUP
    copy = pltpu.make_async_copy(band_ref.at[band, pl.ds(start, PLANE_GROUP)], planes_ref, sem)
    copy.start()
    copy.wait()
    tails = []
    for slot in range(PLANE_GROUP):
        values = planes_ref[slot]
        out_ref[0, slot * N : (slot + 1) * N, :] = values[:, :LANES]
        tails.append(values[:, LANES:])
    tails.append(jnp.zeros((N, LANES - PLANE_GROUP * TAIL), BF16))
    out_ref[0, PLANE_GROUP * N : PACK, :] = jnp.concatenate(tails, axis=1)


def forward_kernel(groups, n_in, me_ref, own_ref, table_ref, *refs):
    low_ref, out_refs = refs[0], refs[1 + n_in :]
    out_refs, (part_ref, tail_ref) = out_refs[:-2], out_refs[-2:]
    z_table, y_table, turned_table = (table_ref[k * 2 * N : (k + 1) * 2 * N, :] for k in range(3))
    for pos, group in enumerate(groups):
        density = []
        for slot in range(PLANE_GROUP):
            lower = plane_of(low_ref, pos, slot)
            density += [own_ref[i, group * PLANE_GROUP + slot].astype(F32) * lower for i in (0, 1)]
        along_z = right(jnp.concatenate(density, axis=0), z_table)
        for slot in range(PLANE_GROUP):
            plane = group * PLANE_GROUP + slot
            pair = [along_z[(slot * 2 + i) * N : (slot * 2 + i + 1) * N] for i in (0, 1)]
            along_y = left(y_table, jnp.concatenate([values[:, :LANES] for values in pair], axis=1))
            for i in (0, 1):
                part_ref[pl.ds(i * X + plane, N, stride=2 * X), :] = along_y[:, i * LANES : (i + 1) * LANES]
                start = (plane * 2 + i) * TAIL
                tail_ref[start : start + TAIL, :] = pair[i][:, LANES:].T
    if not out_refs:
        return
    turned = right(tail_ref[...], turned_table[:, :LANES])
    mask = mask_rows()
    for plane in range(X):
        for i in (0, 1):
            rows = pl.ds(LANES * 2 * X + i * X + plane, TAIL, stride=2 * X)
            start = (plane * 2 + i) * TAIL
            part_ref[rows, :] = jnp.where(mask, part_ref[rows, :], turned[start : start + TAIL])
    store_parts(part_ref, out_refs, me_ref)


def filter_kernel(count, me_ref, kernel_ref, x_ref, x_t_ref, *refs):
    in_refs, out_refs, (part_ref, back_ref) = refs[:count], refs[count:-2], refs[-2:]
    load_parts(in_refs, me_ref, part_ref)
    units = [tuple(range(kind, 2 * X, 4)) for kind in range(4)]
    for unit in units:
        start = X * unit[0] % 8
        kind = start // 2
        columns = []
        for m in unit:
            first = X * m - start
            columns.append(
                jnp.concatenate([part_ref[g * ROWS + first : g * ROWS + first + 24, :] for g in range(GROUPS)], axis=0)
            )
        spectrum = left(x_ref[kind], jnp.concatenate(columns, axis=1))
        spectrum = spectrum * jnp.concatenate([kernel_ref[m // 2] for m in unit], axis=1)
        planes = left(x_t_ref[kind], spectrum)
        for pos, m in enumerate(unit):
            for g in range(GROUPS):
                back_ref[g * ROWS + X * m : g * ROWS + X * (m + 1), :] = planes[
                    g * 24 + start : g * 24 + start + X, pos * LANES : (pos + 1) * LANES
                ]
    store_parts(back_ref, out_refs, me_ref)


def inverse_kernel(groups, count, n_old, me_ref, own_ref, table_ref, *refs):
    refs = list(refs)

    def take(number):
        taken, refs[:number] = refs[:number], []
        return taken

    in_refs, low_refs, old_refs = take(count), take(PLANE_GROUPS if n_old == 0 else 1), take(n_old)
    sum_refs, (back_ref,), (*made, lower_ref) = take(2), take(1), refs
    part_ref, tail_ref = in_refs if count == 2 else made
    z_table, y_table = (table_ref[k * 2 * N : (k + 1) * 2 * N, :] for k in range(2))
    if count != 2:
        load_parts(in_refs, me_ref, part_ref)
        mask = mask_rows()
        high = []
        for plane in range(X):
            for i in (0, 1):
                rows = pl.ds(LANES * 2 * X + i * X + plane, TAIL, stride=2 * X)
                values = part_ref[rows, :]
                part_ref[rows, :] = jnp.where(mask, values, F32(0.0))
                high.append(jnp.where(mask, F32(0.0), values))
        tail_ref[...] = right(jnp.concatenate(high, axis=0), table_ref[4 * N : 4 * N + 2 * LANES, :])

    for pos, group in enumerate(groups):
        low_ref, in_pack = (low_refs[group], 0) if len(low_refs) > 1 else (low_refs[0], group)
        spectra, tails = [], []
        for slot in range(PLANE_GROUP):
            plane = group * PLANE_GROUP + slot
            both = jnp.concatenate(
                [part_ref[pl.ds(i * X + plane, N, stride=2 * X), :] for i in (0, 1)], axis=1
            )
            along_y = left(y_table, both)
            for i in (0, 1):
                start = (plane * 2 + i) * TAIL
                spectra.append(along_y[:, i * LANES : (i + 1) * LANES])
                tails.append(tail_ref[start : start + TAIL, :].T)
        high, low = split(jnp.concatenate(spectra, axis=0))
        tail_high, tail_low = split(jnp.concatenate(tails, axis=0))
        first = mm(jnp.concatenate([high, low], axis=1), jnp.concatenate([z_table[:LANES]] * 2, axis=0))
        second = jnp.concatenate([high, tail_high, tail_low, tail_high], axis=1)
        rest = [z_table[N : N + LANES], z_table[LANES:N], z_table[LANES:N], z_table[N + LANES :]]
        potential = first + mm(second, jnp.concatenate(rest, axis=0))
        largest = jnp.zeros((8, N), F32)
        for slot in range(PLANE_GROUP):
            plane = group * PLANE_GROUP + slot
            lower = plane_of(low_ref, in_pack, slot)
            given = jnp.zeros((N, N), F32)
            for i in (0, 1):
                mine = potential[(slot * 2 + i) * N : (slot * 2 + i + 1) * N]
                given = given - mine * own_ref[i, plane].astype(F32)
                if not old_refs:
                    sum_refs[i][pos * PLANE_GROUP + slot] = -(mine * lower)
                else:
                    sum_refs[i][pos * PLANE_GROUP + slot] = old_refs[i][plane] - mine * lower
            lower_ref[slot] = given
            largest = jnp.maximum(largest, jnp.max(jnp.abs(given).reshape(N // 8, 8, N), axis=0))
        exponent = scale_of(jnp.max(largest, axis=(0, 1), keepdims=True))
        tails = []
        for slot in range(PLANE_GROUP):
            given = lower_ref[slot]
            back_ref[pos, slot * N : (slot + 1) * N, :] = encode(given[:, :LANES], exponent).astype(BF16)
            tails.append(given[:, LANES:])
        tails.append(jnp.zeros((N, LANES - PLANE_GROUP * TAIL), F32))
        back_ref[pos, PLANE_GROUP * N : PACK, :] = encode(jnp.concatenate(tails, axis=1), exponent).astype(BF16)
        back_ref[pos, PACK:BACK, :] = jnp.broadcast_to(exponent, (16, LANES)).astype(BF16)


def add_kernel(count, n_back, *refs):
    sum_refs, back_refs, out_ref = refs[:count], refs[count : count + n_back], refs[-1]
    step = pl.program_id(0)

    def add(sum_ref, back_ref, group):
        exponent = back_ref[group, PACK:BACK, :].astype(F32)[:1, :1]
        high = decode(back_ref[group, PLANE_GROUP * N : PACK, :].astype(F32), exponent)
        for slot in range(PLANE_GROUP):
            main = decode(back_ref[group, slot * N : (slot + 1) * N, :].astype(F32), exponent)
            given = jnp.concatenate([main, high[:, slot * TAIL : (slot + 1) * TAIL]], axis=1)
            out_ref[0, slot] = sum_ref[slot] + given

    for group in range(count):
        back = (back_refs[0], group) if n_back == 1 else (back_refs[group], 0)
        pl.when(step == group)(functools.partial(add, sum_refs[group], *back))


def call(kernel, outs, scratch, rows, me, args, aliases=None):
    specs = [] if me is None else [pl.BlockSpec(memory_space=pltpu.SMEM)]
    me = () if me is None else (me,)
    return pl.pallas_call(
        kernel,
        out_shape=outs,
        in_specs=specs + [pl.BlockSpec(memory_space=pltpu.VMEM)] * len(args),
        scratch_shapes=scratch,
        input_output_aliases=aliases or {},
        compiler_params=pltpu.CompilerParams(vmem_limit_bytes=24 * 2**20),
        cost_estimate=pl.CostEstimate(flops=rows * 2**17, bytes_accessed=2**20, transcendentals=0),
    )(*me, *args)


def pack(orbitals, band, first, count, after):
    return pl.pallas_call(
        functools.partial(pack_kernel, band, first),
        out_shape=jax.ShapeDtypeStruct((count, PACK, LANES), BF16),
        grid=(count,),
        in_specs=[pl.BlockSpec(memory_space=pltpu.HBM)]
        + [pl.BlockSpec(memory_space=pl.ANY)] * len(after),
        out_specs=pl.BlockSpec((1, PACK, LANES), lambda g: (g, 0, 0)),
        scratch_shapes=[pltpu.VMEM((PLANE_GROUP, N, N), BF16), pltpu.SemaphoreType.DMA],
        compiler_params=pltpu.CompilerParams(vmem_limit_bytes=(62 if band == 0 else 24) * 2**20),
        cost_estimate=pl.CostEstimate(flops=count * 2**28, bytes_accessed=2**20, transcendentals=0),
    )(orbitals, *after)


def add_back(band, first, sums, backs, out):
    vmem = pl.BlockSpec(memory_space=pltpu.VMEM)
    count, n_back = len(sums), len(backs)
    return pl.pallas_call(
        functools.partial(add_kernel, count, n_back),
        out_shape=jax.ShapeDtypeStruct((2, X, N, N), F32),
        grid=(count,),
        in_specs=[vmem] * (count + n_back) + [pl.BlockSpec(memory_space=pl.ANY)] * len(out),
        out_specs=pl.BlockSpec((1, PLANE_GROUP, N, N), lambda g: (band, first + g, 0, 0)),
        input_output_aliases={count + n_back: 0} if out else {},
        compiler_params=pltpu.CompilerParams(vmem_limit_bytes=24 * 2**20),
        cost_estimate=pl.CostEstimate(flops=count * 2**28, bytes_accessed=2**20, transcendentals=0),
    )(*sums, *backs, *out)


def shifted(value, axis, steps):
    count = lax.axis_size(axis)
    pairs = [(source, (source + steps) % count) for source in range(count)]
    return lax.ppermute(value, axis, pairs)


def exchange(parts):
    if len(parts) == 1:
        return [lax.all_to_all(parts[0], "grid", split_axis=0, concat_axis=0, tiled=True)]
    received = [parts[0]]
    for part in range(1, GROUPS):
        pairs = [(source, partner(source, part, 1)) for source in range(GROUPS)]
        received.append(lax.ppermute(parts[part], "grid", pairs))
    return received


def body(orbitals):
    table = {name: jnp.asarray(value) for name, value in tables().items()}
    rows = lax.dynamic_slice_in_dim(table["column"], lax.axis_index("grid") * X, X, axis=0)
    kernel = coulomb((table["freq"] ** 2)[None, :, None] + rows[:, None, :])

    back_shape = [jax.ShapeDtypeStruct((count, BACK, LANES), BF16) for count in (1, PLANE_GROUPS)]
    sent_shape = {1: [jax.ShapeDtypeStruct((GROUPS, SENT, LANES), BF16)]}
    sent_shape[GROUPS] = [jax.ShapeDtypeStruct((SENT, LANES), BF16)] * GROUPS
    part_shape = jax.ShapeDtypeStruct((GROUPS * ROWS, LANES), F32)
    tail_shape = jax.ShapeDtypeStruct((2 * X * TAIL, N), F32)
    planes_shape = jax.ShapeDtypeStruct((PLANE_GROUP, N, N), F32)
    sum_shape = jax.ShapeDtypeStruct((X, N, N), F32)
    part, tail, planes = (pltpu.VMEM(shape.shape, F32) for shape in (part_shape, tail_shape, planes_shape))
    me = lax.axis_index("grid").astype(jnp.int32).reshape(1)
    every = tuple(range(PLANE_GROUPS))

    packed, lower = [], []
    with jax.named_scope("pack"):
        for group in every:
            packed.append(pack(orbitals, 0, group, 1, packed[-1:]))
            lower.append(shifted(packed[-1], "band", 1))
    own = lax.optimization_barrier((orbitals, packed[-1]))[0]
    with jax.named_scope("forward"):
        made = []
        for group in every[:-1]:
            made = call(
                functools.partial(forward_kernel, (group,), len(made)), [part_shape, tail_shape], [], 20000, me,
                [own, table["yz"], lower[group], *made], {4: 0, 5: 1} if made else {},
            )
            if group == 0:
                moved = shifted(pack(orbitals, 1, 0, PLANE_GROUPS, made[1:]), "band", 1)
        *first_forth, _, _ = call(
            functools.partial(forward_kernel, every[-1:], 2), [*sent_shape[FORTH[0]], part_shape, tail_shape], [],
            20000, me, [own, table["yz"], lower[-1], *made], {4: FORTH[0], 5: FORTH[0] + 1},
        )
        second_forth = call(
            functools.partial(forward_kernel, every, 0), sent_shape[FORTH[1]], [part, tail], 60000, me,
            [own, table["yz"], moved],
        )
    spectra = [list(lax.optimization_barrier((exchange(first_forth), list(second_forth)))[0])]
    filtered = []
    for j in (0, 1):
        with jax.named_scope("filter"):
            sent = call(
                functools.partial(filter_kernel, FORTH[j]), sent_shape[BACKWARD[j]], [part, part], 60000, me,
                [kernel, table["x"], table["x_t"], *spectra[j]],
            )
            if j == 0:
                late = lax.optimization_barrier((list(second_forth[LATE:]), list(sent)))[0]
                spectra.append(exchange([*second_forth[:LATE], *late]))
            filtered.append(exchange(sent))
    with jax.named_scope("inverse"):
        *older, first_back = call(
            functools.partial(inverse_kernel, every, BACKWARD[0], 0), [sum_shape] * 2 + [back_shape[1]],
            [part, tail, planes], 60000, me, [own, table["yz_t"], *filtered[0], *lower],
        )
        first_back = shifted(first_back, "band", -1)
        sums, second_back = [], []
        for group in every:
            shapes = [planes_shape] * 2 + [back_shape[0]]
            if group == 0:
                *results, part_out, tail_out = call(
                    functools.partial(inverse_kernel, (group,), BACKWARD[1], 2), [*shapes, part_shape, tail_shape],
                    [planes], 30000, me, [own, table["yz_t"], *filtered[1], moved, *older],
                )
            else:
                results = call(
                    functools.partial(inverse_kernel, (group,), 2, 2), shapes, [planes], 20000, me,
                    [own, table["yz_t"], part_out, tail_out, moved, *older],
                )
            sums.append(results[:2])
            second_back.append(shifted(results[2], "band", -1))
    with jax.named_scope("add"):
        out = add_back(0, 0, [pair[0] for pair in sums], [first_back], [])
        out = add_back(1, 0, [pair[1] for pair in sums[:-1]], second_back[:-1], [out])
        return add_back(1, PLANE_GROUPS - 1, [sums[-1][1]], second_back[-1:], [out])


def solution(mesh):
    in_specs = (P("band", "grid", None, None),)
    out_specs = P("band", "grid", None, None)
    return jax.shard_map(body, mesh=mesh, in_specs=in_specs, out_specs=out_specs, check_vma=False)
```

```python
import functools
import math

import jax
import jax.numpy as jnp
import ml_dtypes
import numpy as np
from jax import lax
from jax.experimental import pallas as pl
from jax.experimental.pallas import tpu as pltpu
from jax.sharding import PartitionSpec as P

OMEGA = 0.5
N = 144
HALF = N // 2
GROUPS = 8
X = N // GROUPS
LANES = 128
TAIL = N - LANES
ROWS = X * 2 * X
SENT = ROWS + 8
POWER = 12.0
PLANE_GROUP = 6
PLANE_GROUPS = X // PLANE_GROUP
PACK = (PLANE_GROUP + 1) * N
BACK = PACK + 16
FORTH = (GROUPS, GROUPS)
BACKWARD = (GROUPS, GROUPS)
LATE = 5
F32 = jnp.float32
BF16 = jnp.bfloat16


def real_basis():
    freq = np.array([0] + [f for f in range(1, HALF) for _ in (0, 1)] + [HALF])
    points = np.arange(N)
    rows = []
    for idx, f in enumerate(freq):
        angle = 2.0 * np.pi * ((f * points) % N) / N
        if f in (0, HALF):
            rows.append(np.cos(angle) / np.sqrt(N))
        else:
            rows.append((np.cos(angle) if idx % 2 else np.sin(angle)) * np.sqrt(2.0 / N))
    return np.array(rows), freq


def z_order():
    return np.array(list(range(LANES)) + [N - 1] + list(range(LANES, N - 1)))


def main_mask():
    lane = np.arange(LANES)[None, :]
    row = np.arange(TAIL)[:, None]
    return lane < np.where(row == 0, 65, 63)


def column_freq_sq():
    freq = real_basis()[1]
    z_freq = freq[z_order()]
    sq = freq[:, None] ** 2 + z_freq[None, :LANES] ** 2
    turned = z_freq[LANES:, None] ** 2 + freq[LANES - 1 - np.arange(LANES)][None, :] ** 2
    sq[LANES:] = np.where(main_mask(), sq[LANES:], turned)
    return sq.astype(np.int32)


def split_const(values):
    high = values.astype(ml_dtypes.bfloat16)
    low = (values - high.astype(np.float64)).astype(ml_dtypes.bfloat16)
    return high, low


def stacked(values):
    return np.concatenate(split_const(values), axis=0)


@functools.cache
def tables():
    basis, freq = real_basis()
    z_basis = basis[z_order()]
    turned = np.zeros((N, LANES))
    turned[:, 63:] = basis[64::-1].T
    x_in, x_out = [], []
    for off in (0, 2, 4, 6):
        padded = np.zeros((N, GROUPS, 24))
        padded[:, :, off : off + X] = basis.reshape(N, GROUPS, X)
        padded = padded.reshape(N, GROUPS * 24)
        x_in.append(stacked(padded))
        x_out.append(stacked(padded.T))
    return {
        "yz": np.concatenate([stacked(z_basis.T), stacked(basis), stacked(np.pad(turned, ((0, 0), (0, TAIL))))]),
        "yz_t": np.concatenate([stacked(z_basis), stacked(basis.T), stacked(turned.T)]),
        "x": np.stack(x_in),
        "x_t": np.stack(x_out),
        "freq": freq.astype(np.int32),
        "column": column_freq_sq(),
    }


def coulomb(freq_sq):
    g_sq = freq_sq.astype(F32) * F32((2.0 * math.pi / N) ** 2)
    safe_sq = jnp.where(freq_sq > 0, g_sq, F32(1.0))
    values = jnp.where(
        freq_sq > 0,
        4.0 * math.pi / safe_sq * -jnp.expm1(-safe_sq / (4.0 * OMEGA * OMEGA)),
        F32(math.pi / (OMEGA * OMEGA)),
    )
    return jnp.where(freq_sq <= HALF**2, values, F32(0.0))


def mm(a, b):
    return lax.dot_general(a, b, (((1,), (0,)), ((), ())), preferred_element_type=F32)


def split(values):
    high = values.astype(BF16)
    return high, (values - high.astype(F32)).astype(BF16)


def right(values, table):
    rows = table.shape[0] // 2
    high, low = split(values)
    if rows == LANES:
        return mm(high, table[:rows]) + mm(high, table[rows:]) + mm(low, table[:rows])
    first = mm(
        jnp.concatenate([high[:, :LANES], low[:, :LANES]], axis=1),
        jnp.concatenate([table[:LANES], table[:LANES]], axis=0),
    )
    second = jnp.concatenate([high, low[:, LANES:], high[:, LANES:]], axis=1)
    return first + mm(
        second,
        jnp.concatenate([table[rows : rows + LANES], table[LANES:rows], table[LANES:rows], table[rows + LANES :]], axis=0),
    )


def left(table, values):
    rows = table.shape[0] // 2
    high, low = split(values)
    both = mm(table, high)
    return both[:rows] + both[rows:] + mm(table[:rows], low)


def scale_of(largest):
    return jnp.floor(10.0 - jnp.log(jnp.maximum(largest, F32(2.0**-60))) * F32(1.0 / math.log(2.0)))


def encode(values, exponent):
    scaled = values * jnp.exp2(exponent)
    fourth = scaled * scaled
    fourth = fourth * fourth
    twelfth = fourth * fourth * fourth
    return jnp.where(values < 0, -twelfth, twelfth)


def decode(codes, exponent):
    size = jnp.exp2(jnp.log(jnp.abs(codes)) * F32(1.0 / math.log(2.0) / POWER) - exponent)
    return jnp.where(codes < 0, -size, size)


def partner(me, part, sign):
    return (me // 4 + part // 4) % 2 * 4 + (me % 4 + sign * (part % 4) + 4) % 4


def largest_of(values):
    return jnp.max(jnp.abs(values), axis=(0, 1), keepdims=True)


def store_parts(part_ref, out_refs, me_ref):
    starts = [part * ROWS for part in range(GROUPS)]
    if len(out_refs) > 1:
        starts = [pl.multiple_of(partner(me_ref[0], part, 1) * ROWS, 8) for part in range(GROUPS)]
    sizes = [
        jnp.max(jnp.abs(part_ref[pl.ds(start, ROWS), :]).reshape(ROWS // 8, 8, LANES), axis=0) for start in starts
    ]
    sizes = jnp.concatenate([jnp.max(values, axis=0, keepdims=True) for values in sizes], axis=0)
    exponents = scale_of(jnp.max(sizes, axis=1, keepdims=True))
    for part, start in enumerate(starts):
        exponent = exponents[part : part + 1]
        codes = encode(part_ref[pl.ds(start, ROWS), :], exponent)
        codes = jnp.concatenate([codes, jnp.broadcast_to(exponent, (8, LANES))], axis=0).astype(BF16)
        if len(out_refs) > 1:
            out_refs[part][...] = codes
        else:
            out_refs[0][part] = codes


def load_parts(in_refs, me_ref, part_ref):
    for part in range(GROUPS):
        if len(in_refs) > 1:
            codes, source = in_refs[part][...], partner(me_ref[0], part, -1)
        else:
            codes, source = in_refs[0][part], part
        codes = codes.astype(F32)
        start = pl.multiple_of(source * ROWS, 8) if len(in_refs) > 1 else source * ROWS
        part_ref[pl.ds(start, ROWS), :] = decode(codes[:ROWS], codes[ROWS : ROWS + 1])


def plane_of(pack_ref, group, slot):
    high = pack_ref[group, PLANE_GROUP * N : PACK, :].astype(F32)
    main = pack_ref[group, slot * N : (slot + 1) * N, :].astype(F32)
    return jnp.concatenate([main, high[:, slot * TAIL : (slot + 1) * TAIL]], axis=1)


def mask_rows():
    lane = lax.broadcasted_iota(jnp.int32, (TAIL, LANES), 1)
    row = lax.broadcasted_iota(jnp.int32, (TAIL, LANES), 0)
    return lane < jnp.where(row == 0, 65, 63)


def pack_kernel(band, first, band_ref, *refs):
    out_ref, planes_ref, sem = refs[-3:]
    start = (first + pl.program_id(0)) * PLANE_GROUP
    copies = [
        pltpu.make_async_copy(band_ref.at[band, start + slot], planes_ref.at[slot], sem.at[slot])
        for slot in range(PLANE_GROUP)
    ]
    for copy in copies:
        copy.start()
    tails = []
    for slot in range(PLANE_GROUP):
        copies[slot].wait()
        values = planes_ref[slot]
        out_ref[0, slot * N : (slot + 1) * N, :] = values[:, :LANES]
        tails.append(values[:, LANES:])
    tails.append(jnp.zeros((N, LANES - PLANE_GROUP * TAIL), BF16))
    out_ref[0, PLANE_GROUP * N : PACK, :] = jnp.concatenate(tails, axis=1)


def forward_kernel(groups, n_in, me_ref, own_ref, table_ref, *refs):
    low_ref, out_refs = refs[0], refs[1 + n_in :]
    out_refs, (part_ref, tail_ref) = out_refs[:-2], out_refs[-2:]
    z_table, y_table, turned_table = (table_ref[k * 2 * N : (k + 1) * 2 * N, :] for k in range(3))
    for pos, group in enumerate(groups):
        density = []
        for slot in range(PLANE_GROUP):
            lower = plane_of(low_ref, pos, slot)
            density += [own_ref[i, group * PLANE_GROUP + slot].astype(F32) * lower for i in (0, 1)]
        along_z = right(jnp.concatenate(density, axis=0), z_table)
        for slot in range(PLANE_GROUP):
            plane = group * PLANE_GROUP + slot
            pair = [along_z[(slot * 2 + i) * N : (slot * 2 + i + 1) * N] for i in (0, 1)]
            along_y = left(y_table, jnp.concatenate([values[:, :LANES] for values in pair], axis=1))
            for i in (0, 1):
                part_ref[pl.ds(i * X + plane, N, stride=2 * X), :] = along_y[:, i * LANES : (i + 1) * LANES]
                start = (plane * 2 + i) * TAIL
                tail_ref[start : start + TAIL, :] = pair[i][:, LANES:].T
    if not out_refs:
        return
    turned = right(tail_ref[...], turned_table[:, :LANES])
    mask = mask_rows()
    for plane in range(X):
        for i in (0, 1):
            rows = pl.ds(LANES * 2 * X + i * X + plane, TAIL, stride=2 * X)
            start = (plane * 2 + i) * TAIL
            part_ref[rows, :] = jnp.where(mask, part_ref[rows, :], turned[start : start + TAIL])
    store_parts(part_ref, out_refs, me_ref)


def filter_kernel(count, me_ref, kernel_ref, x_ref, x_t_ref, *refs):
    in_refs, out_refs, (part_ref, back_ref) = refs[:count], refs[count:-2], refs[-2:]
    load_parts(in_refs, me_ref, part_ref)
    units = [tuple(range(kind, 2 * X, 4)) for kind in range(4)]
    for unit in units:
        start = X * unit[0] % 8
        kind = start // 2
        columns = []
        for m in unit:
            first = X * m - start
            columns.append(
                jnp.concatenate([part_ref[g * ROWS + first : g * ROWS + first + 24, :] for g in range(GROUPS)], axis=0)
            )
        spectrum = left(x_ref[kind], jnp.concatenate(columns, axis=1))
        spectrum = spectrum * jnp.concatenate([kernel_ref[m // 2] for m in unit], axis=1)
        planes = left(x_t_ref[kind], spectrum)
        for pos, m in enumerate(unit):
            for g in range(GROUPS):
                back_ref[g * ROWS + X * m : g * ROWS + X * (m + 1), :] = planes[
                    g * 24 + start : g * 24 + start + X, pos * LANES : (pos + 1) * LANES
                ]
    store_parts(back_ref, out_refs, me_ref)


def inverse_kernel(groups, count, n_old, me_ref, own_ref, table_ref, *refs):
    refs = list(refs)

    def take(number):
        taken, refs[:number] = refs[:number], []
        return taken

    in_refs, low_refs, old_refs = take(count), take(PLANE_GROUPS if n_old == 0 else 1), take(n_old)
    sum_refs, (back_ref,), (*made, lower_ref) = take(2), take(1), refs
    part_ref, tail_ref = in_refs if count == 2 else made
    z_table, y_table = (table_ref[k * 2 * N : (k + 1) * 2 * N, :] for k in range(2))
    if count != 2:
        load_parts(in_refs, me_ref, part_ref)
        mask = mask_rows()
        high = []
        for plane in range(X):
            for i in (0, 1):
                rows = pl.ds(LANES * 2 * X + i * X + plane, TAIL, stride=2 * X)
                values = part_ref[rows, :]
                part_ref[rows, :] = jnp.where(mask, values, F32(0.0))
                high.append(jnp.where(mask, F32(0.0), values))
        tail_ref[...] = right(jnp.concatenate(high, axis=0), table_ref[4 * N : 4 * N + 2 * LANES, :])

    for pos, group in enumerate(groups):
        low_ref, in_pack = (low_refs[group], 0) if len(low_refs) > 1 else (low_refs[0], group)
        spectra, tails = [], []
        for slot in range(PLANE_GROUP):
            plane = group * PLANE_GROUP + slot
            both = jnp.concatenate(
                [part_ref[pl.ds(i * X + plane, N, stride=2 * X), :] for i in (0, 1)], axis=1
            )
            along_y = left(y_table, both)
            for i in (0, 1):
                start = (plane * 2 + i) * TAIL
                spectra.append(along_y[:, i * LANES : (i + 1) * LANES])
                tails.append(tail_ref[start : start + TAIL, :].T)
        high, low = split(jnp.concatenate(spectra, axis=0))
        tail_high, tail_low = split(jnp.concatenate(tails, axis=0))
        first = mm(jnp.concatenate([high, low], axis=1), jnp.concatenate([z_table[:LANES]] * 2, axis=0))
        second = jnp.concatenate([high, tail_high, tail_low, tail_high], axis=1)
        rest = [z_table[N : N + LANES], z_table[LANES:N], z_table[LANES:N], z_table[N + LANES :]]
        potential = first + mm(second, jnp.concatenate(rest, axis=0))
        largest = jnp.zeros((8, N), F32)
        for slot in range(PLANE_GROUP):
            plane = group * PLANE_GROUP + slot
            lower = plane_of(low_ref, in_pack, slot)
            given = jnp.zeros((N, N), F32)
            for i in (0, 1):
                mine = potential[(slot * 2 + i) * N : (slot * 2 + i + 1) * N]
                given = given - mine * own_ref[i, plane].astype(F32)
                if not old_refs:
                    sum_refs[i][pos * PLANE_GROUP + slot] = -(mine * lower)
                else:
                    sum_refs[i][pos * PLANE_GROUP + slot] = old_refs[i][plane] - mine * lower
            lower_ref[slot] = given
            largest = jnp.maximum(largest, jnp.max(jnp.abs(given).reshape(N // 8, 8, N), axis=0))
        exponent = scale_of(jnp.max(largest, axis=(0, 1), keepdims=True))
        tails = []
        for slot in range(PLANE_GROUP):
            given = lower_ref[slot]
            back_ref[pos, slot * N : (slot + 1) * N, :] = encode(given[:, :LANES], exponent).astype(BF16)
            tails.append(given[:, LANES:])
        tails.append(jnp.zeros((N, LANES - PLANE_GROUP * TAIL), F32))
        back_ref[pos, PLANE_GROUP * N : PACK, :] = encode(jnp.concatenate(tails, axis=1), exponent).astype(BF16)
        back_ref[pos, PACK:BACK, :] = jnp.broadcast_to(exponent, (16, LANES)).astype(BF16)


def add_kernel(count, n_back, *refs):
    sum_refs, back_refs, out_ref = refs[:count], refs[count : count + n_back], refs[-1]
    step = pl.program_id(0)

    def add(sum_ref, back_ref, group):
        exponent = back_ref[group, PACK:BACK, :].astype(F32)[:1, :1]
        high = decode(back_ref[group, PLANE_GROUP * N : PACK, :].astype(F32), exponent)
        for slot in range(PLANE_GROUP):
            main = decode(back_ref[group, slot * N : (slot + 1) * N, :].astype(F32), exponent)
            given = jnp.concatenate([main, high[:, slot * TAIL : (slot + 1) * TAIL]], axis=1)
            out_ref[0, slot] = sum_ref[slot] + given

    for group in range(count):
        back = (back_refs[0], group) if n_back == 1 else (back_refs[group], 0)
        pl.when(step == group)(functools.partial(add, sum_refs[group], *back))


def call(kernel, outs, scratch, rows, me, args, aliases=None):
    specs = [] if me is None else [pl.BlockSpec(memory_space=pltpu.SMEM)]
    me = () if me is None else (me,)
    return pl.pallas_call(
        kernel,
        out_shape=outs,
        in_specs=specs + [pl.BlockSpec(memory_space=pltpu.VMEM)] * len(args),
        scratch_shapes=scratch,
        input_output_aliases=aliases or {},
        compiler_params=pltpu.CompilerParams(vmem_limit_bytes=24 * 2**20),
        cost_estimate=pl.CostEstimate(flops=rows * 2**17, bytes_accessed=2**20, transcendentals=0),
    )(*me, *args)


def pack(orbitals, band, first, count, after):
    return pl.pallas_call(
        functools.partial(pack_kernel, band, first),
        out_shape=jax.ShapeDtypeStruct((count, PACK, LANES), BF16),
        grid=(count,),
        in_specs=[pl.BlockSpec(memory_space=pltpu.HBM)]
        + [pl.BlockSpec(memory_space=pl.ANY)] * len(after),
        out_specs=pl.BlockSpec((1, PACK, LANES), lambda g: (g, 0, 0)),
        scratch_shapes=[pltpu.VMEM((PLANE_GROUP, N, N), BF16), pltpu.SemaphoreType.DMA((PLANE_GROUP,))],
        compiler_params=pltpu.CompilerParams(vmem_limit_bytes=(62 if band == 0 else 24) * 2**20),
        cost_estimate=pl.CostEstimate(flops=count * 2**28, bytes_accessed=2**20, transcendentals=0),
    )(orbitals, *after)


def add_back(band, first, sums, backs, out):
    vmem = pl.BlockSpec(memory_space=pltpu.VMEM)
    count, n_back = len(sums), len(backs)
    return pl.pallas_call(
        functools.partial(add_kernel, count, n_back),
        out_shape=jax.ShapeDtypeStruct((2, X, N, N), F32),
        grid=(count,),
        in_specs=[vmem] * (count + n_back) + [pl.BlockSpec(memory_space=pl.ANY)] * len(out),
        out_specs=pl.BlockSpec((1, PLANE_GROUP, N, N), lambda g: (band, first + g, 0, 0)),
        input_output_aliases={count + n_back: 0} if out else {},
        compiler_params=pltpu.CompilerParams(vmem_limit_bytes=24 * 2**20),
        cost_estimate=pl.CostEstimate(flops=count * 2**28, bytes_accessed=2**20, transcendentals=0),
    )(*sums, *backs, *out)


def shifted(value, axis, steps):
    count = lax.axis_size(axis)
    pairs = [(source, (source + steps) % count) for source in range(count)]
    return lax.ppermute(value, axis, pairs)


def exchange(parts):
    if len(parts) == 1:
        return [lax.all_to_all(parts[0], "grid", split_axis=0, concat_axis=0, tiled=True)]
    received = [parts[0]]
    for part in range(1, GROUPS):
        pairs = [(source, partner(source, part, 1)) for source in range(GROUPS)]
        received.append(lax.ppermute(parts[part], "grid", pairs))
    return received


def body(orbitals):
    table = {name: jnp.asarray(value) for name, value in tables().items()}
    rows = lax.dynamic_slice_in_dim(table["column"], lax.axis_index("grid") * X, X, axis=0)
    kernel = coulomb((table["freq"] ** 2)[None, :, None] + rows[:, None, :])

    back_shape = [jax.ShapeDtypeStruct((count, BACK, LANES), BF16) for count in (1, PLANE_GROUPS)]
    sent_shape = {1: [jax.ShapeDtypeStruct((GROUPS, SENT, LANES), BF16)]}
    sent_shape[GROUPS] = [jax.ShapeDtypeStruct((SENT, LANES), BF16)] * GROUPS
    part_shape = jax.ShapeDtypeStruct((GROUPS * ROWS, LANES), F32)
    tail_shape = jax.ShapeDtypeStruct((2 * X * TAIL, N), F32)
    planes_shape = jax.ShapeDtypeStruct((PLANE_GROUP, N, N), F32)
    sum_shape = jax.ShapeDtypeStruct((X, N, N), F32)
    part, tail, planes = (pltpu.VMEM(shape.shape, F32) for shape in (part_shape, tail_shape, planes_shape))
    me = lax.axis_index("grid").astype(jnp.int32).reshape(1)
    every = tuple(range(PLANE_GROUPS))

    packed, lower = [], []
    with jax.named_scope("pack"):
        for group in every:
            packed.append(pack(orbitals, 0, group, 1, packed[-1:]))
            lower.append(shifted(packed[-1], "band", 1))
    own = lax.optimization_barrier((orbitals, packed[-1]))[0]
    with jax.named_scope("forward"):
        made = []
        for group in every[:-1]:
            made = call(
                functools.partial(forward_kernel, (group,), len(made)), [part_shape, tail_shape], [], 20000, me,
                [own, table["yz"], lower[group], *made], {4: 0, 5: 1} if made else {},
            )
            if group == 0:
                moved = shifted(pack(orbitals, 1, 0, PLANE_GROUPS, made[1:]), "band", 1)
        *first_forth, _, _ = call(
            functools.partial(forward_kernel, every[-1:], 2), [*sent_shape[FORTH[0]], part_shape, tail_shape], [],
            20000, me, [own, table["yz"], lower[-1], *made], {4: FORTH[0], 5: FORTH[0] + 1},
        )
        second_forth = call(
            functools.partial(forward_kernel, every, 0), sent_shape[FORTH[1]], [part, tail], 60000, me,
            [own, table["yz"], moved],
        )
    spectra = [list(lax.optimization_barrier((exchange(first_forth), list(second_forth)))[0])]
    filtered = []
    for j in (0, 1):
        with jax.named_scope("filter"):
            sent = call(
                functools.partial(filter_kernel, FORTH[j]), sent_shape[BACKWARD[j]], [part, part], 60000, me,
                [kernel, table["x"], table["x_t"], *spectra[j]],
            )
            if j == 0:
                late = lax.optimization_barrier((list(second_forth[LATE:]), list(sent)))[0]
                spectra.append(exchange([*second_forth[:LATE], *late]))
            filtered.append(exchange(sent))
    with jax.named_scope("inverse"):
        *older, first_back = call(
            functools.partial(inverse_kernel, every, BACKWARD[0], 0), [sum_shape] * 2 + [back_shape[1]],
            [part, tail, planes], 60000, me, [own, table["yz_t"], *filtered[0], *lower],
        )
        first_back = shifted(first_back, "band", -1)
        sums, second_back = [], []
        for group in every:
            shapes = [planes_shape] * 2 + [back_shape[0]]
            if group == 0:
                *results, part_out, tail_out = call(
                    functools.partial(inverse_kernel, (group,), BACKWARD[1], 2), [*shapes, part_shape, tail_shape],
                    [planes], 30000, me, [own, table["yz_t"], *filtered[1], moved, *older],
                )
            else:
                results = call(
                    functools.partial(inverse_kernel, (group,), 2, 2), shapes, [planes], 20000, me,
                    [own, table["yz_t"], part_out, tail_out, moved, *older],
                )
            sums.append(results[:2])
            second_back.append(shifted(results[2], "band", -1))
    with jax.named_scope("add"):
        out = add_back(0, 0, [pair[0] for pair in sums], [first_back], [])
        out = add_back(1, 0, [pair[1] for pair in sums[:-1]], second_back[:-1], [out])
        return add_back(1, PLANE_GROUPS - 1, [sums[-1][1]], second_back[-1:], [out])


def solution(mesh):
    in_specs = (P("band", "grid", None, None),)
    out_specs = P("band", "grid", None, None)
    return jax.shard_map(body, mesh=mesh, in_specs=in_specs, out_specs=out_specs, check_vma=False)
```
